256 devices in a mesh: grp: 4 (over z_lo), wide: 64 (over z_hi, y, x, core).
Axes of the slice: x: 4, y: 4, z: 8 (z_hi: 2, z_lo: 4; z = z_hi * 4 + z_lo), core: 2. Of those that a mesh axis runs over, the one named last changes fastest.
Arguments:
- plan: float32 [8192, 32768], P('grp', 'wide'), may hold values from 0.1 to 10
- cost_source: float32 [8192, 1536], P(('grp', 'wide')), may hold values from -52 to 52
- cost_target: float32 [32768, 1024], P('wide', 'grp'), may hold values from -42 to 42
- potential_col: float32 [1024], replicated, may hold values from -12 to 12
- row_mass: float32 [1536], P(('grp', 'wide')), may hold values from 0.5 to 2
Outputs:
- gradient: float32 [1536, 1024], P(('grp', 'wide'))
- potential_row: float32 [1536], P(('grp', 'wide'))
The draws below stay inside these ranges and needn't reach their ends.
All inputs are finite; a program needn't handle non-finite values.
Results may differ from the reference program's by a relative error of at most 0.00012.
Values sent between devices are 32-bit elements; how exact they have to be, the bound alone decides.
No kernel may reach another device: no remote copies, remote signals or barrier semaphores. Data moves between devices by JAX's collectives and lax.ppermute only.
A program may use at most 64 MiB of HBM per device.

```python
import math
import jax
import jax.numpy as jnp
from jax import lax

WR = 1536
WC = 1024
NS = 8192
NT = 32768


def draw_cost_source(key, part):
    key = jax.random.fold_in(key, 11)
    return jnp.clip(jax.random.normal(key, (NS, WR), jnp.float32), -6.0, 6.0)


def draw_cost_target(key, part):
    key = jax.random.fold_in(key, 23)
    return jnp.clip(jax.random.normal(key, (NT, WC), jnp.float32), -6.0, 6.0)


def block_scale(stream_key, dims, shards, least, top_value):
    def one(position, shards_of):
        steps = jax.random.uniform(jax.random.fold_in(jax.random.fold_in(stream_key, 6), position), (shards_of,), jnp.float32, least / len(shards), top_value / len(shards))
        return jnp.repeat(jnp.exp(steps), dims[position] // shards_of).reshape((-1,) + (1,) * (len(dims) - position - 1))

    level = one(*shards[0])
    for cut in shards[1:]:
        level = level * one(*cut)
    return level


def gaussian(rng, dims, width, limit, dtype=jnp.bfloat16):
    return jnp.clip(width * jax.random.normal(rng, dims, jnp.float32), -limit, limit).astype(dtype)


def setup_inputs(seed: int = 0) -> dict:
    streams_of = jax.random.split(jax.random.key(seed), 6)
    return {
        "plan": jnp.clip(jnp.exp(math.log(10.0) - 4.6051702 * jax.random.uniform(streams_of[0], (NS, NT), jnp.float32) ** block_scale(streams_of[0], (NS, NT), ((0, 4), (1, 64)), -0.2, 0.2)), 0.1, 10.0),
        "cost_source": draw_cost_source(jax.random.fold_in(streams_of[5], 71), 0),
        "cost_target": draw_cost_target(jax.random.fold_in(streams_of[5], 71), 0),
        "potential_col": gaussian(streams_of[3], (WC,), 2.0, 12.0, jnp.float32),
        "row_mass": jnp.clip(jnp.exp(math.log(2.0) - 1.3862944 * jax.random.uniform(streams_of[4], (WR,), jnp.float32) ** block_scale(streams_of[4], (WR,), ((0, 256),), -0.2, 0.2)), 0.5, 2.0),
    }


entropy = 2.0

def reference(plan, cost_source, cost_target, potential_col, row_mass):
    highest = lax.Precision.HIGHEST
    carried = jnp.dot(plan, cost_target, precision=highest)
    factor = -2.0 / math.sqrt(NS * NT)
    gradient = factor * jnp.dot(cost_source.T, carried, precision=highest)
    scores = (potential_col[None, :] - gradient) / entropy
    peak = lax.optimization_barrier(jnp.max(scores, axis=1, keepdims=True))
    log_total = peak[:, 0] + jnp.log(lax.optimization_barrier(jnp.sum(jnp.exp(scores - peak), axis=1)))
    potential_row = entropy * jnp.log(row_mass) - entropy * log_total
    return (gradient, potential_row)
```

```python
import math

import jax
import jax.numpy as jnp
from jax import lax
from jax.experimental import pallas as pl
from jax.experimental.pallas import tpu as pltpu
from jax.sharding import PartitionSpec as P

entropy = 2.0
NX = NY = 4
NC = 2
NH = 2
NG = 4
WIDE = NH * NY * NX * NC


def coords(w):
    return w // (NY * NX * NC), (w // (NX * NC)) % NY, (w // NC) % NX, w % NC


def wide_index(h, y, x, c):
    return ((h * NY + y % NY) * NX + x % NX) * NC + c


def wide_pairs(move):
    return [(w, wide_index(*move(*coords(w)))) for w in range(WIDE)]


def first_pairs(d):
    return wide_pairs(lambda h, y, x, c: (h, y, x + d, c) if c == 0 else (h, y + d, x, c))


def second_pairs(d):
    return wide_pairs(lambda h, y, x, c: (h, y + d, x, c) if c == 0 else (h, y, x + d, c))


CORE_SWAP = wide_pairs(lambda h, y, x, c: (h, y, x, 1 - c))
H_SWAP = wide_pairs(lambda h, y, x, c: (1 - h, y, x, c))


def y_pairs(d):
    return wide_pairs(lambda h, y, x, c: (h, y + d, x, c))


def halves(v):
    hi = v.astype(jnp.bfloat16)
    return hi, (v - hi.astype(jnp.float32)).astype(jnp.bfloat16)


def dot3(a, b):
    (ah, al), (bh, bl) = a, b

    def dot(u, v):
        return jnp.dot(u, v, preferred_element_type=jnp.float32)

    return dot(ah, bh) + (dot(ah, bl) + dot(al, bh))


def carry_kernel(place, *refs, n_blocks):
    plan_ref, blocks, (own_ref, send_ref) = refs[0], refs[1 : 1 + n_blocks], refs[1 + n_blocks :]
    c, x, y = place[0], place[1], place[2]
    xx = pl.program_id(0)
    rows = plan_ref[...].reshape(-1, plan_ref.shape[-1])
    block = blocks[0][...]
    for other in blocks[1:]:
        block = block + other[...]
    out = dot3(halves(rows), halves(block)).T
    part = out.shape[0] // (NC * NY)
    for cc in range(NC):
        for yy in range(NY):
            chunk = out[(cc * NY + yy) * part : (cc * NY + yy + 1) * part, :]
            dx, dy = lax.rem(xx - x + NX, NX), lax.rem(yy - y + NY, NY)
            d1, d2 = (dx, dy) if cc == 0 else (dy, dx)

            @pl.when(c == cc)
            def _():
                own_ref[d1, d2] = chunk

            @pl.when(c != cc)
            def _():
                send_ref[d1, d2] = chunk


def carry(place, plan5, blocks):
    groups, nx, run, depth = plan5.shape
    cols = blocks[0].shape[1]
    part = cols // (NC * NY)
    out = jax.ShapeDtypeStruct((4, 4, part, groups * run), jnp.float32)
    whole = pl.BlockSpec(out.shape, lambda i, s: (0, 0, 0, 0))
    return pl.pallas_call(
        lambda place, *refs: carry_kernel(place, *refs, n_blocks=len(blocks)),
        grid_spec=pltpu.PrefetchScalarGridSpec(
            num_scalar_prefetch=1,
            grid=(nx,),
            in_specs=[pl.BlockSpec((groups, 1, run, depth), lambda i, s: (0, i, 0, 0))]
            + [pl.BlockSpec(b.shape, lambda i, s: (0, 0)) for b in blocks],
            out_specs=[whole, whole],
        ),
        out_shape=[out, out],
        compiler_params=pltpu.CompilerParams(vmem_limit_bytes=32 * 1024 * 1024),
        cost_estimate=pl.CostEstimate(
            flops=6 * groups * nx * run * depth * cols, bytes_accessed=4 * 1024 * 1024, transcendentals=0
        ),
        name="carry",
    )(place, plan5, *blocks)


def grad_kernel(place, *refs, factor):
    pieces, blocks, out_ref, cost, held = refs[:4], refs[4:8], refs[8], refs[9], refs[10]
    c, y, h, g = place[0], place[2], place[3], place[4]
    run = pieces[0].shape[1]
    for dh in range(NH):
        for dc in range(NC):
            for d in range(NY):
                hh = lax.rem(h + dh, NH)
                cc = lax.rem(c + dc, NC)
                yy = lax.rem(y - d + NY, NY)
                at = pl.multiple_of(((hh * NY + yy) * NC + cc) * run, run)
                cost[pl.ds(at, run), :] = pieces[dh * NC + dc][d]
    part = blocks[0].shape[0]
    low = g < 2
    order = [g, g + 1 - 2 * lax.rem(g, 2), jnp.where(low, 2, 1), jnp.where(low, 3, 0)]
    for j, block in zip(order, blocks, strict=True):
        held[pl.ds(pl.multiple_of(j * part, part), part), :] = block[...]
    left = halves(held[...])
    step = 512
    for at in range(0, cost.shape[1], step):
        out = dot3(left, halves(cost[:, at : at + step]))
        out_ref[at : at + step, :] = factor * out.T


def grad(place, pieces, blocks, factor):
    rows = NH * NC * NY * pieces[0].shape[1]
    width = pieces[0].shape[2]
    cols = 4 * blocks[0].shape[0]
    vmem = pl.BlockSpec(memory_space=pltpu.VMEM)
    return pl.pallas_call(
        lambda place, *refs: grad_kernel(place, *refs, factor=factor),
        in_specs=[pl.BlockSpec(memory_space=pltpu.SMEM)] + [vmem] * 8,
        out_specs=vmem,
        out_shape=jax.ShapeDtypeStruct((width, cols), jnp.float32),
        scratch_shapes=[pltpu.VMEM((rows, width), jnp.float32), pltpu.VMEM((cols, rows), jnp.float32)],
        compiler_params=pltpu.CompilerParams(vmem_limit_bytes=32 * 1024 * 1024),
        cost_estimate=pl.CostEstimate(flops=6 * rows * width * cols, bytes_accessed=4 * 1024 * 1024, transcendentals=0),
        name="grad",
    )(place, *pieces, *blocks)


def after(value, *others):
    return lax.optimization_barrier((value, *others))[0]


def body(plan, cost_source, cost_target, potential_col, row_mass):
    num_source = plan.shape[0] * NG
    num_target = plan.shape[1] * WIDE
    factor = -2.0 / math.sqrt(num_source * num_target)
    g = lax.axis_index("grp")
    w = lax.axis_index("wide")
    h, y, x, c = coords(w)
    place = jnp.stack([c, x, y, h, g]).astype(jnp.int32)
    run = NC * cost_source.shape[0]
    plan5 = plan.reshape(NH * NY, NX, run, plan.shape[1])

    def wide(v, pairs):
        return lax.ppermute(v, "wide", pairs)

    pair = lax.ppermute(cost_target, "grp", [(0, 1), (1, 0), (2, 3), (3, 2)])
    mid1 = lax.ppermute(cost_target, "grp", [(1, 2), (2, 1)])
    mid2 = lax.ppermute(pair, "grp", [(1, 2), (2, 1)])
    end1 = lax.ppermute(mid1, "grp", [(1, 0), (2, 3)])
    end2 = lax.ppermute(mid2, "grp", [(1, 0), (2, 3)])

    def gather_y(v):
        piece = jnp.stack([v] + [wide(v, y_pairs(d)) for d in (1, 2, 3)])
        return piece, wide(piece, CORE_SWAP)

    def exchange(blocks):
        own, send = carry(place, plan5, blocks)
        got = wide(send, CORE_SWAP)
        parts = [own[d] + got[d] for d in range(4)]
        return parts[0] + sum(wide(parts[d], first_pairs(d)) for d in (1, 2, 3))

    def finish(total):
        return total[0] + sum(wide(total[d], second_pairs(d)) for d in (1, 2, 3))

    pieces = gather_y(cost_source)
    done = [finish(exchange(blocks)) for blocks in ((cost_target,), (pair,), (mid1, end1), (mid2, end2))]
    far = wide(after(cost_source, end2), H_SWAP)
    pieces += gather_y(far)
    partial = grad(place, pieces, done, factor)

    n_all = NG * WIDE
    rows = partial.shape[0] // n_all
    parts = lax.all_to_all(partial.reshape(n_all, rows, -1), ("grp", "wide"), 0, 0, tiled=True)
    parts = parts.reshape(NG, NH, NY, NX, NC, rows, 4, -1)
    summed = parts.sum(axis=(0, 1, 3))
    gradient = summed.transpose(2, 3, 1, 0, 4).reshape(rows, -1)

    scores = (potential_col[None, :] - gradient) / entropy
    peak = jnp.max(scores, axis=1, keepdims=True)
    log_total = peak[:, 0] + jnp.log(jnp.sum(jnp.exp(scores - peak), axis=1))
    potential_row = entropy * jnp.log(row_mass) - entropy * log_total
    return (gradient, potential_row)


def solution(mesh):
    placed = (P("grp", "wide"), P(("grp", "wide"), None), P("wide", "grp"), P(), P(("grp", "wide")))
    return jax.shard_map(
        body,
        mesh=mesh,
        in_specs=placed,
        out_specs=(P(("grp", "wide"), None), P(("grp", "wide"))),
        check_vma=False,
    )
```

```python
import math

import jax
import jax.numpy as jnp
from jax import lax
from jax.experimental import pallas as pl
from jax.experimental.pallas import tpu as pltpu
from jax.sharding import PartitionSpec as P

entropy = 2.0
NX = NY = 4
NC = 2
NH = 2
NG = 4
WIDE = NH * NY * NX * NC
MIB = 1024 * 1024
BIG = 10**11


def coords(w):
    return w // (NY * NX * NC), (w // (NX * NC)) % NY, (w // NC) % NX, w % NC


def wide_index(h, y, x, c):
    return ((h * NY + y % NY) * NX + x % NX) * NC + c


def wide_pairs(move):
    return [(w, wide_index(*move(*coords(w)))) for w in range(WIDE)]


def row_pairs(d):
    return wide_pairs(lambda h, y, x, c: (h, y, x + d, c) if c == 0 else (h, y + d, x, c))


def column_pairs(d):
    return wide_pairs(lambda h, y, x, c: (h, y + d, x, c) if c == 0 else (h, y, x + d, c))


CORE_SWAP = wide_pairs(lambda h, y, x, c: (h, y, x, 1 - c))
H_SWAP = wide_pairs(lambda h, y, x, c: (1 - h, y, x, c))
GATHER_GROUPS = [
    [
        g * WIDE + (wide_index(h, b, a, 0) if c == 0 else wide_index(h, a, b, 1))
        for g in range(NG)
        for h in range(NH)
        for b in range(4)
    ]
    for c in range(NC)
    for a in range(4)
]


def halves(v):
    hi = v.astype(jnp.bfloat16)
    return hi, (v - hi.astype(jnp.float32)).astype(jnp.bfloat16)


def dot3(a, b):
    def dot(u, v):
        return jnp.dot(u, v, preferred_element_type=jnp.float32)

    return dot(a[0], b[0]) + (dot(a[0], b[1]) + dot(a[1], b[0]))


def params():
    return pltpu.CompilerParams(vmem_limit_bytes=40 * MIB)


COST = pl.CostEstimate(flops=1000, bytes_accessed=1000, transcendentals=0)
VMEM = pl.BlockSpec(memory_space=pltpu.VMEM)
SMEM = pl.BlockSpec(memory_space=pltpu.SMEM)


def split_kernel(place, plan_ref, hi_ref, lo_ref):
    h = place[3]
    groups, nx, run, depth = plan_ref.shape
    per = groups // NH
    for xx in range(nx):
        for dh in range(NH):
            for i in range(per):
                hi, lo = halves(plan_ref[lax.rem(h + dh, NH) * per + i, xx])
                at = (dh * per + i) * run
                hi_ref[xx, at : at + run, :] = hi
                lo_ref[xx, at : at + run, :] = lo


def split(place, plan5):
    groups, nx, run, depth = plan5.shape
    out = jax.ShapeDtypeStruct((nx, groups * run, depth), jnp.bfloat16)
    return pl.pallas_call(
        split_kernel,
        in_specs=[SMEM, VMEM],
        out_specs=[VMEM, VMEM],
        out_shape=[out, out],
        compiler_params=params(),
        cost_estimate=COST,
        name="split",
    )(place, plan5)


def carry_kernel(place, hi_ref, lo_ref, *refs):
    blocks, (own_ref, send_ref, held) = refs[:-3], refs[-3:]
    c, x, y = place[0], place[1], place[2]
    nx, rows, _ = hi_ref.shape
    per = rows // (NH * NY)

    def put(cc, d1, d2, n, chunk):
        @pl.when(c == cc)
        def _():
            own_ref[d1, d2, n] = chunk

        @pl.when(c != cc)
        def _():
            send_ref[d1, d2, n] = chunk

    for n, block in enumerate(blocks):
        right = halves(block[...])
        half = block.shape[1] // NC
        part = half // 4

        def step(xx, carried):
            out = dot3((hi_ref[xx], lo_ref[xx]), right)
            low = out[:, :half].T
            for yy in range(NY):
                put(0, lax.rem(xx - x + NX, NX), lax.rem(yy - y + NY, NY), n, low[yy * part : (yy + 1) * part])
            for i in range(NH * NY):
                held[i, xx] = out[i * per : (i + 1) * per, half:]
            return carried

        lax.fori_loop(0, nx, step, 0)
        for yy in range(NY):
            piece = [held[dh * NY + yy].reshape(nx * per, half) for dh in range(NH)]
            high = jnp.concatenate(piece, axis=0).T
            for xo in range(NX):
                put(1, lax.rem(yy - y + NY, NY), lax.rem(xo - x + NX, NX), n, high[xo * part : (xo + 1) * part])


def carry(place, plan, blocks, flops):
    nx, rows, _ = plan[0].shape
    cols = blocks[0].shape[1]
    out = jax.ShapeDtypeStruct((4, 4, len(blocks), cols // (NC * 4), rows), jnp.float32)
    return pl.pallas_call(
        carry_kernel,
        in_specs=[SMEM, VMEM, VMEM] + [VMEM] * len(blocks),
        out_specs=[VMEM, VMEM],
        out_shape=[out, out],
        scratch_shapes=[pltpu.VMEM((NH * NY, nx, rows // (NH * NY), cols // NC), jnp.float32)],
        compiler_params=params(),
        cost_estimate=pl.CostEstimate(flops=flops, bytes_accessed=1000, transcendentals=0),
        name="carry",
    )(place, *plan, *blocks)


def grad_kernel(place, *refs, factor):
    pieces, (blocks, out_ref, cost, held, full) = refs[:4], refs[4:]
    c, x, y, g = place[0], place[1], place[2], place[4]
    a, b = jnp.where(c == 0, x, y), jnp.where(c == 0, y, x)
    run = pieces[0].shape[1]
    for d in range(4):
        bb = lax.rem(b - d + 4, 4)
        for dc in range(NC):
            at = (bb * NC + lax.rem(c + dc, NC)) * run
            cost[pl.ds(pl.multiple_of(at, run), run), :] = pieces[d][dc]
    part = blocks.shape[1]
    low, even = g < 2, lax.rem(g, 2) == 0
    near = jnp.where(even, g + 1, g - 1)
    order = [g, near, jnp.where(low, g + 2, g - 2), jnp.where(low, near + 2, near - 2)]
    for k, j in enumerate(order):
        held[pl.ds(pl.multiple_of(j * part, part), part), :] = blocks[k]
    left = halves(held[...])
    step = 512
    width = cost.shape[1]
    for at in range(0, width, step):
        full[at : at + step, :] = factor * dot3(left, halves(cost[:, at : at + step])).T
    full[width:, :] = jnp.zeros((full.shape[0] - width, full.shape[1]), jnp.float32)
    chips = NG * NH * NY * NX
    rows = width // chips
    pad = out_ref.shape[2]
    for cc in range(NC):

        @pl.when(c == cc)
        def _(cc=cc):
            for o in range(chips):
                gh, yy, xx = o // (NY * NX), (o // NX) % NY, o % NX
                aa, bb = (xx, yy) if cc == 0 else (yy, xx)
                out_ref[lax.rem(aa - a + 4, 4), gh * 4 + bb] = full[o * rows : o * rows + pad, :]


def grad(place, pieces, blocks, factor):
    _, run, width = pieces[0].shape
    rows = NC * 4 * run
    cols = blocks.shape[0] * blocks.shape[1]
    pad = -(-width // (NG * NH * NY * NX) // 8) * 8
    return pl.pallas_call(
        lambda place, *refs: grad_kernel(place, *refs, factor=factor),
        in_specs=[SMEM] + [VMEM] * 5,
        out_specs=VMEM,
        out_shape=jax.ShapeDtypeStruct((4, NG * NH * 4, pad, cols), jnp.float32),
        scratch_shapes=[
            pltpu.VMEM((rows, width), jnp.float32),
            pltpu.VMEM((cols, rows), jnp.float32),
            pltpu.VMEM((width + 8, cols), jnp.float32),
        ],
        compiler_params=params(),
        cost_estimate=COST,
        name="grad",
    )(place, *pieces, blocks)


def arrange_kernel(place, own, got, potential, out_ref, log_ref):
    c = place[0]
    rows = out_ref.shape[0]

    def mine(v):
        return jnp.where(c == 0, v[:, :rows, :], v[:, rows : 2 * rows, :])

    mine_own, mine_got = mine(own), mine(got)
    low = jnp.where(c == 0, mine_own, mine_got)
    high = jnp.where(c == 0, mine_got, mine_own)
    part = own.shape[2] // 4
    pieces = [v[b, :, j * part : (j + 1) * part] for j in range(4) for v in (low, high) for b in range(4)]
    gradient = jnp.concatenate(pieces, axis=1)
    out_ref[...] = gradient
    scores = (potential[...] - gradient) / entropy
    peak = jnp.max(scores, axis=1, keepdims=True)
    total = jnp.sum(jnp.exp(scores - peak), axis=1, keepdims=True)
    log_ref[...] = peak + jnp.log(total)


def arrange(place, own, got, potential, rows):
    return pl.pallas_call(
        arrange_kernel,
        in_specs=[SMEM, VMEM, VMEM, VMEM],
        out_specs=[VMEM, VMEM],
        out_shape=[
            jax.ShapeDtypeStruct((rows, potential.shape[1]), jnp.float32),
            jax.ShapeDtypeStruct((rows, 1), jnp.float32),
        ],
        compiler_params=params(),
        cost_estimate=COST,
        name="arrange",
    )(place, own, got, potential)


def meet_kernel(*refs):
    refs[-1][...] = jnp.zeros_like(refs[-1])


def meet(flops, width, *arrays):
    return pl.pallas_call(
        meet_kernel,
        in_specs=[pl.BlockSpec(memory_space=pl.ANY)] * len(arrays),
        out_specs=VMEM,
        out_shape=jax.ShapeDtypeStruct((1, width), jnp.float32),
        compiler_params=params(),
        cost_estimate=pl.CostEstimate(flops=flops, bytes_accessed=1000, transcendentals=0),
        name="meet",
    )(*arrays)


def after(value, *others):
    return lax.optimization_barrier((value, *others))[0]


def body(plan, cost_source, cost_target, potential_col, row_mass):
    num_source = plan.shape[0] * NG
    num_target = plan.shape[1] * WIDE
    factor = -2.0 / math.sqrt(num_source * num_target)
    g = lax.axis_index("grp")
    w = lax.axis_index("wide")
    h, y, x, c = coords(w)
    place = jnp.stack([c, x, y, h, g]).astype(jnp.int32)
    plan5 = plan.reshape(NH * NY, NX, NC * cost_source.shape[0], plan.shape[1])

    def wide(v, pairs):
        return lax.ppermute(v, "wide", pairs)

    both = jnp.stack([cost_source, wide(cost_source, CORE_SWAP)])
    costs = [wide(both, column_pairs(d)) for d in (1, 2, 3)]
    halved = split(place, plan5)

    def along_rows(own, got):
        parts = [own[d] + got[d] for d in range(4)]
        return parts[0] + sum(wide(parts[d], row_pairs(d)) for d in (1, 2, 3))

    def finish(total):
        total = total[0] + sum(wide(total[d], column_pairs(d)) for d in (1, 2, 3))
        rows = total.shape[-1] // NH
        return total[..., :rows] + wide(total[..., rows:], H_SWAP)

    near = lax.ppermute(cost_target, "grp", [(i, i ^ 1) for i in range(NG)])
    far = lax.ppermute(cost_target, "grp", [(i, i ^ 2) for i in range(NG)])
    own0, send0 = carry(place, halved, (cost_target,), 1000)
    got0 = wide(send0, CORE_SWAP) + meet(BIG, own0.shape[-1], own0, far, *costs)
    last = lax.ppermute(far, "grp", [(i, i ^ 1) for i in range(NG)])
    total0 = along_rows(own0, got0)
    own1, send1 = carry(place, halved, (near, far), BIG)
    total1 = along_rows(own1, wide(send1, CORE_SWAP))
    own2, send2 = carry(place, halved, (after(last, total0),), BIG)
    total2 = along_rows(own2, wide(send2, CORE_SWAP)) + meet(1000, own0.shape[-1], total1)
    blocks = finish(jnp.concatenate([total0, total1, total2], axis=1))

    partial = grad(place, [both] + costs, blocks, factor)
    partial = partial[0] + sum(wide(partial[d], row_pairs(d)) for d in (1, 2, 3))
    parts = lax.all_to_all(partial, ("grp", "wide"), 0, 0, axis_index_groups=GATHER_GROUPS, tiled=True)
    summed = parts.reshape((NG * NH, 4) + parts.shape[1:]).sum(axis=0)
    gradient, log_total = arrange(place, summed, wide(summed, CORE_SWAP), potential_col[None, :], row_mass.shape[0])
    potential_row = entropy * jnp.log(row_mass) - entropy * log_total[:, 0]
    return (gradient, potential_row)


def solution(mesh):
    placed = (P("grp", "wide"), P(("grp", "wide"), None), P("wide", "grp"), P(), P(("grp", "wide")))
    return jax.shard_map(
        body,
        mesh=mesh,
        in_specs=placed,
        out_specs=(P(("grp", "wide"), None), P(("grp", "wide"))),
        check_vma=False,
    )
```

```python
import math

import jax
import jax.numpy as jnp
from jax import lax
from jax.experimental import pallas as pl
from jax.experimental.pallas import tpu as pltpu
from jax.sharding import PartitionSpec as P

entropy = 2.0
NX = NY = 4
NC = 2
NH = 2
NG = 4
WIDE = NH * NY * NX * NC
MIB = 1024 * 1024
BIG = 10**11


def coords(w):
    return w // (NY * NX * NC), (w // (NX * NC)) % NY, (w // NC) % NX, w % NC


def wide_index(h, y, x, c):
    return ((h * NY + y % NY) * NX + x % NX) * NC + c


def wide_pairs(move):
    return [(w, wide_index(*move(*coords(w)))) for w in range(WIDE)]


def row_pairs(d):
    return wide_pairs(lambda h, y, x, c: (h, y, x + d, c) if c == 0 else (h, y + d, x, c))


def column_pairs(d):
    return wide_pairs(lambda h, y, x, c: (h, y + d, x, c) if c == 0 else (h, y, x + d, c))


CORE_SWAP = wide_pairs(lambda h, y, x, c: (h, y, x, 1 - c))
H_SWAP = wide_pairs(lambda h, y, x, c: (1 - h, y, x, c))
GATHER_GROUPS = [
    [
        g * WIDE + (wide_index(h, b, a, 0) if c == 0 else wide_index(h, a, b, 1))
        for g in range(NG)
        for h in range(NH)
        for b in range(4)
    ]
    for c in range(NC)
    for a in range(4)
]


def halves(v):
    hi = v.astype(jnp.bfloat16)
    return hi, (v - hi.astype(jnp.float32)).astype(jnp.bfloat16)


def dot3(a, b):
    def dot(u, v):
        return jnp.dot(u, v, preferred_element_type=jnp.float32)

    return dot(a[0], b[0]) + (dot(a[0], b[1]) + dot(a[1], b[0]))


def params():
    return pltpu.CompilerParams(vmem_limit_bytes=40 * MIB)


COST = pl.CostEstimate(flops=1000, bytes_accessed=1000, transcendentals=0)
VMEM = pl.BlockSpec(memory_space=pltpu.VMEM)
SMEM = pl.BlockSpec(memory_space=pltpu.SMEM)


def split_kernel(place, plan_ref, hi_ref, lo_ref):
    h = place[3]
    groups, nx, run, depth = plan_ref.shape
    per = groups // NH
    for xx in range(nx):
        for dh in range(NH):
            for i in range(per):
                hi, lo = halves(plan_ref[lax.rem(h + dh, NH) * per + i, xx])
                at = (dh * per + i) * run
                hi_ref[xx, at : at + run, :] = hi
                lo_ref[xx, at : at + run, :] = lo


def split(place, plan5):
    groups, nx, run, depth = plan5.shape
    out = jax.ShapeDtypeStruct((nx, groups * run, depth), jnp.bfloat16)
    return pl.pallas_call(
        split_kernel,
        in_specs=[SMEM, VMEM],
        out_specs=[VMEM, VMEM],
        out_shape=[out, out],
        compiler_params=params(),
        cost_estimate=COST,
        name="split",
    )(place, plan5)


def carry_kernel(place, hi_ref, lo_ref, *refs):
    blocks, (own_ref, send_ref, held) = refs[:-3], refs[-3:]
    c, x, y = place[0], place[1], place[2]
    nx, rows, _ = hi_ref.shape
    per = rows // (NH * NY)
    for n, block in enumerate(blocks):
        right = halves(block[...])
        half = block.shape[1] // NC
        part = half // 4
        for xx in range(nx):
            out = dot3((hi_ref[xx], lo_ref[xx]), right)
            for i in range(NH * NY):
                held[n, i, xx] = out[i * per : (i + 1) * per]
        for ref, core in ((own_ref, c), (send_ref, 1 - c)):
            a, b = jnp.where(core == 0, x, y), jnp.where(core == 0, y, x)
            lanes = pl.ds(pl.multiple_of(core * half, half), half)
            for i in range(4):
                tiles = []
                for dh in range(NH):
                    for j in range(4):
                        yy, xx = jnp.where(core == 0, j, i), jnp.where(core == 0, i, j)
                        tiles.append(held[n, dh * NY + yy, xx, :, lanes])
                turned = jnp.concatenate(tiles, axis=0).T
                for j in range(4):
                    ref[lax.rem(i - a + 4, 4), lax.rem(j - b + 4, 4), n] = turned[j * part : (j + 1) * part]
def carry(place, plan, blocks, flops):
    nx, rows, _ = plan[0].shape
    cols = blocks[0].shape[1]
    out = jax.ShapeDtypeStruct((4, 4, len(blocks), cols // (NC * 4), rows), jnp.float32)
    return pl.pallas_call(
        carry_kernel,
        in_specs=[SMEM, VMEM, VMEM] + [VMEM] * len(blocks),
        out_specs=[VMEM, VMEM],
        out_shape=[out, out],
        scratch_shapes=[pltpu.VMEM((len(blocks), NH * NY, nx, rows // (NH * NY), cols), jnp.float32)],
        compiler_params=params(),
        cost_estimate=pl.CostEstimate(flops=flops, bytes_accessed=1000, transcendentals=0),
        name="carry",
    )(place, *plan, *blocks)


def grad_kernel(place, *refs, factor):
    pieces, (blocks, out_ref, cost, held, full) = refs[:4], refs[4:]
    c, x, y, g = place[0], place[1], place[2], place[4]
    a, b = jnp.where(c == 0, x, y), jnp.where(c == 0, y, x)
    run = pieces[0].shape[1]
    for d in range(4):
        bb = lax.rem(b - d + 4, 4)
        for dc in range(NC):
            at = (bb * NC + lax.rem(c + dc, NC)) * run
            cost[pl.ds(pl.multiple_of(at, run), run), :] = pieces[d][dc]
    part = blocks.shape[1]
    low, even = g < 2, lax.rem(g, 2) == 0
    near = jnp.where(even, g + 1, g - 1)
    order = [g, near, jnp.where(low, g + 2, g - 2), jnp.where(low, near + 2, near - 2)]
    for k, j in enumerate(order):
        held[pl.ds(pl.multiple_of(j * part, part), part), :] = blocks[k]
    left = halves(held[...])
    step = 512
    width = cost.shape[1]
    for at in range(0, width, step):
        full[at : at + step, :] = factor * dot3(left, halves(cost[:, at : at + step])).T
    full[width:, :] = jnp.zeros((full.shape[0] - width, full.shape[1]), jnp.float32)
    chips = NG * NH * NY * NX
    rows = width // chips
    pad = out_ref.shape[2]
    for cc in range(NC):

        @pl.when(c == cc)
        def _(cc=cc):
            for o in range(chips):
                gh, yy, xx = o // (NY * NX), (o // NX) % NY, o % NX
                aa, bb = (xx, yy) if cc == 0 else (yy, xx)
                out_ref[lax.rem(aa - a + 4, 4), gh * 4 + bb] = full[o * rows : o * rows + pad, :]


def grad(place, pieces, blocks, factor):
    _, run, width = pieces[0].shape
    rows = NC * 4 * run
    cols = blocks.shape[0] * blocks.shape[1]
    pad = -(-width // (NG * NH * NY * NX) // 8) * 8
    return pl.pallas_call(
        lambda place, *refs: grad_kernel(place, *refs, factor=factor),
        in_specs=[SMEM] + [VMEM] * 5,
        out_specs=VMEM,
        out_shape=jax.ShapeDtypeStruct((4, NG * NH * 4, pad, cols), jnp.float32),
        scratch_shapes=[
            pltpu.VMEM((rows, width), jnp.float32),
            pltpu.VMEM((cols, rows), jnp.float32),
            pltpu.VMEM((width + 8, cols), jnp.float32),
        ],
        compiler_params=params(),
        cost_estimate=COST,
        name="grad",
    )(place, *pieces, blocks)


def arrange_kernel(place, own, got, potential, out_ref, log_ref):
    c = place[0]
    rows = out_ref.shape[0]

    def mine(v):
        return jnp.where(c == 0, v[:, :rows, :], v[:, rows : 2 * rows, :])

    mine_own, mine_got = mine(own), mine(got)
    low = jnp.where(c == 0, mine_own, mine_got)
    high = jnp.where(c == 0, mine_got, mine_own)
    part = own.shape[2] // 4
    pieces = [v[b, :, j * part : (j + 1) * part] for j in range(4) for v in (low, high) for b in range(4)]
    gradient = jnp.concatenate(pieces, axis=1)
    out_ref[...] = gradient
    scores = (potential[...] - gradient) / entropy
    peak = jnp.max(scores, axis=1, keepdims=True)
    total = jnp.sum(jnp.exp(scores - peak), axis=1, keepdims=True)
    log_ref[...] = peak + jnp.log(total)


def arrange(place, own, got, potential, rows):
    return pl.pallas_call(
        arrange_kernel,
        in_specs=[SMEM, VMEM, VMEM, VMEM],
        out_specs=[VMEM, VMEM],
        out_shape=[
            jax.ShapeDtypeStruct((rows, potential.shape[1]), jnp.float32),
            jax.ShapeDtypeStruct((rows, 1), jnp.float32),
        ],
        compiler_params=params(),
        cost_estimate=COST,
        name="arrange",
    )(place, own, got, potential)


def meet_kernel(*refs):
    refs[-1][...] = jnp.zeros_like(refs[-1])


def meet(flops, width, *arrays):
    return pl.pallas_call(
        meet_kernel,
        in_specs=[pl.BlockSpec(memory_space=pl.ANY)] * len(arrays),
        out_specs=VMEM,
        out_shape=jax.ShapeDtypeStruct((1, width), jnp.float32),
        compiler_params=params(),
        cost_estimate=pl.CostEstimate(flops=flops, bytes_accessed=1000, transcendentals=0),
        name="meet",
    )(*arrays)


def after(value, *others):
    return lax.optimization_barrier((value, *others))[0]


def body(plan, cost_source, cost_target, potential_col, row_mass):
    num_source = plan.shape[0] * NG
    num_target = plan.shape[1] * WIDE
    factor = -2.0 / math.sqrt(num_source * num_target)
    g = lax.axis_index("grp")
    w = lax.axis_index("wide")
    h, y, x, c = coords(w)
    place = jnp.stack([c, x, y, h, g]).astype(jnp.int32)
    plan5 = plan.reshape(NH * NY, NX, NC * cost_source.shape[0], plan.shape[1])

    def wide(v, pairs):
        return lax.ppermute(v, "wide", pairs)

    both = jnp.stack([cost_source, wide(cost_source, CORE_SWAP)])
    costs = [wide(both, column_pairs(d)) for d in (1, 2, 3)]
    halved = split(place, plan5)

    def along_rows(own, got):
        parts = [own[d] + got[d] for d in range(4)]
        return parts[0] + sum(wide(parts[d], row_pairs(d)) for d in (1, 2, 3))

    def finish(total):
        total = total[0] + sum(wide(total[d], column_pairs(d)) for d in (1, 2, 3))
        rows = total.shape[-1] // NH
        return total[..., :rows] + wide(total[..., rows:], H_SWAP)

    near = lax.ppermute(cost_target, "grp", [(i, i ^ 1) for i in range(NG)])
    far = lax.ppermute(cost_target, "grp", [(i, i ^ 2) for i in range(NG)])
    own0, send0 = carry(place, halved, (cost_target,), 1000)
    got0 = wide(send0, CORE_SWAP) + meet(BIG, own0.shape[-1], own0, far, *costs)
    last = lax.ppermute(far, "grp", [(i, i ^ 1) for i in range(NG)])
    total0 = along_rows(own0, got0)
    own1, send1 = carry(place, halved, (near, far), BIG)
    total1 = along_rows(own1, wide(send1, CORE_SWAP))
    own2, send2 = carry(place, halved, (after(last, total0),), BIG)
    total2 = along_rows(own2, wide(send2, CORE_SWAP)) + meet(1000, own0.shape[-1], total1)
    blocks = finish(jnp.concatenate([total0, total1, total2], axis=1))

    partial = grad(place, [both] + costs, blocks, factor)
    partial = partial[0] + sum(wide(partial[d], row_pairs(d)) for d in (1, 2, 3))
    parts = lax.all_to_all(partial, ("grp", "wide"), 0, 0, axis_index_groups=GATHER_GROUPS, tiled=True)
    summed = parts.reshape((NG * NH, 4) + parts.shape[1:]).sum(axis=0)
    gradient, log_total = arrange(place, summed, wide(summed, CORE_SWAP), potential_col[None, :], row_mass.shape[0])
    potential_row = entropy * jnp.log(row_mass) - entropy * log_total[:, 0]
    return (gradient, potential_row)


def solution(mesh):
    placed = (P("grp", "wide"), P(("grp", "wide"), None), P("wide", "grp"), P(), P(("grp", "wide")))
    return jax.shard_map(
        body,
        mesh=mesh,
        in_specs=placed,
        out_specs=(P(("grp", "wide"), None), P(("grp", "wide"))),
        check_vma=False,
    )
```

```python
import math

import jax
import jax.numpy as jnp
from jax import lax
from jax.experimental import pallas as pl
from jax.experimental.pallas import tpu as pltpu
from jax.sharding import PartitionSpec as P

entropy = 2.0
NX = NY = 4
NC = 2
NH = 2
NG = 4
WIDE = NH * NY * NX * NC
MIB = 1024 * 1024
BIG = 10**11


def coords(w):
    return w // (NY * NX * NC), (w // (NX * NC)) % NY, (w // NC) % NX, w % NC


def wide_index(h, y, x, c):
    return ((h * NY + y % NY) * NX + x % NX) * NC + c


def wide_pairs(move):
    return [(w, wide_index(*move(*coords(w)))) for w in range(WIDE)]


def row_pairs(d):
    return wide_pairs(lambda h, y, x, c: (h, y, x + d, c) if c == 0 else (h, y + d, x, c))


def column_pairs(d):
    return wide_pairs(lambda h, y, x, c: (h, y + d, x, c) if c == 0 else (h, y, x + d, c))


CORE_SWAP = wide_pairs(lambda h, y, x, c: (h, y, x, 1 - c))
H_SWAP = wide_pairs(lambda h, y, x, c: (1 - h, y, x, c))
GATHER_GROUPS = [
    [
        g * WIDE + (wide_index(h, b, a, 0) if c == 0 else wide_index(h, a, b, 1))
        for g in range(NG)
        for h in range(NH)
        for b in range(4)
    ]
    for c in range(NC)
    for a in range(4)
]


def halves(v):
    hi = v.astype(jnp.bfloat16)
    return hi, (v - hi.astype(jnp.float32)).astype(jnp.bfloat16)


def dot3(a, b):
    def dot(u, v):
        return jnp.dot(u, v, preferred_element_type=jnp.float32)

    return dot(a[0], b[0]) + (dot(a[0], b[1]) + dot(a[1], b[0]))


def params():
    return pltpu.CompilerParams(vmem_limit_bytes=40 * MIB)


COST = pl.CostEstimate(flops=1000, bytes_accessed=1000, transcendentals=0)
VMEM = pl.BlockSpec(memory_space=pltpu.VMEM)
SMEM = pl.BlockSpec(memory_space=pltpu.SMEM)


def split_kernel(place, plan_ref, hi_ref, lo_ref):
    h = place[3]
    groups, nx, run, depth = plan_ref.shape
    per = groups // NH
    for xx in range(nx):
        for dh in range(NH):
            for i in range(per):
                hi, lo = halves(plan_ref[lax.rem(h + dh, NH) * per + i, xx])
                at = (dh * per + i) * run
                hi_ref[xx, at : at + run, :] = hi
                lo_ref[xx, at : at + run, :] = lo


def split(place, plan5):
    groups, nx, run, depth = plan5.shape
    out = jax.ShapeDtypeStruct((nx, groups * run, depth), jnp.bfloat16)
    return pl.pallas_call(
        split_kernel,
        in_specs=[SMEM, VMEM],
        out_specs=[VMEM, VMEM],
        out_shape=[out, out],
        compiler_params=params(),
        cost_estimate=COST,
        name="split",
    )(place, plan5)


def carry_kernel(place, hi_ref, lo_ref, *refs):
    blocks, (own_ref, send_ref, held) = refs[:-3], refs[-3:]
    c, x, y = place[0], place[1], place[2]
    nx, rows, _ = hi_ref.shape
    per = rows // (NH * NY)
    for n, block in enumerate(blocks):
        right = halves(block[...])
        half = block.shape[1] // NC
        part = half // 4
        for xx in range(nx):
            out = dot3((hi_ref[xx], lo_ref[xx]), right)
            for i in range(NH * NY):
                held[n, i, xx] = out[i * per : (i + 1) * per]
        for ref, core in ((own_ref, c), (send_ref, 1 - c)):
            a, b = jnp.where(core == 0, x, y), jnp.where(core == 0, y, x)
            lanes = pl.ds(pl.multiple_of(core * half, half), half)
            for i in range(4):
                tiles = []
                for dh in range(NH):
                    for j in range(4):
                        yy, xx = jnp.where(core == 0, j, i), jnp.where(core == 0, i, j)
                        tiles.append(held[n, dh * NY + yy, xx, :, lanes])
                turned = jnp.concatenate(tiles, axis=0).T
                for j in range(4):
                    ref[lax.rem(i - a + 4, 4), lax.rem(j - b + 4, 4), n] = turned[j * part : (j + 1) * part]
def carry(place, plan, blocks, flops):
    nx, rows, _ = plan[0].shape
    cols = blocks[0].shape[1]
    out = jax.ShapeDtypeStruct((4, 4, len(blocks), cols // (NC * 4), rows), jnp.float32)
    return pl.pallas_call(
        carry_kernel,
        in_specs=[SMEM, VMEM, VMEM] + [VMEM] * len(blocks),
        out_specs=[VMEM, VMEM],
        out_shape=[out, out],
        scratch_shapes=[pltpu.VMEM((len(blocks), NH * NY, nx, rows // (NH * NY), cols), jnp.float32)],
        compiler_params=params(),
        cost_estimate=pl.CostEstimate(flops=flops, bytes_accessed=1000, transcendentals=0),
        name="carry",
    )(place, *plan, *blocks)


def grad_kernel(place, *refs, factor):
    pieces, (blocks, out_ref, cost, held, full) = refs[:4], refs[4:]
    c, x, y, g = place[0], place[1], place[2], place[4]
    a, b = jnp.where(c == 0, x, y), jnp.where(c == 0, y, x)
    run = pieces[0].shape[1]
    for d in range(4):
        bb = lax.rem(b - d + 4, 4)
        for dc in range(NC):
            at = (bb * NC + lax.rem(c + dc, NC)) * run
            cost[pl.ds(pl.multiple_of(at, run), run), :] = pieces[d][dc]
    part = blocks.shape[1]
    low, even = g < 2, lax.rem(g, 2) == 0
    near = jnp.where(even, g + 1, g - 1)
    order = [g, near, jnp.where(low, g + 2, g - 2), jnp.where(low, near + 2, near - 2)]
    for k, j in enumerate(order):
        held[pl.ds(pl.multiple_of(j * part, part), part), :] = blocks[k]
    left = halves(held[...])
    step = 512
    width = cost.shape[1]
    for at in range(0, width, step):
        full[at : at + step, :] = factor * dot3(left, halves(cost[:, at : at + step])).T
    full[width:, :] = jnp.zeros((full.shape[0] - width, full.shape[1]), jnp.float32)
    chips = NG * NH * NY * NX
    rows = width // chips
    pad = out_ref.shape[2]
    for cc in range(NC):

        @pl.when(c == cc)
        def _(cc=cc):
            for o in range(chips):
                gh, yy, xx = o // (NY * NX), (o // NX) % NY, o % NX
                aa, bb = (xx, yy) if cc == 0 else (yy, xx)
                out_ref[lax.rem(aa - a + 4, 4), gh * 4 + bb] = full[o * rows : o * rows + pad, :]


def grad(place, pieces, blocks, factor):
    _, run, width = pieces[0].shape
    rows = NC * 4 * run
    cols = blocks.shape[0] * blocks.shape[1]
    pad = -(-width // (NG * NH * NY * NX) // 8) * 8
    return pl.pallas_call(
        lambda place, *refs: grad_kernel(place, *refs, factor=factor),
        in_specs=[SMEM] + [VMEM] * 5,
        out_specs=VMEM,
        out_shape=jax.ShapeDtypeStruct((4, NG * NH * 4, pad, cols), jnp.float32),
        scratch_shapes=[
            pltpu.VMEM((rows, width), jnp.float32),
            pltpu.VMEM((cols, rows), jnp.float32),
            pltpu.VMEM((width + 8, cols), jnp.float32),
        ],
        compiler_params=params(),
        cost_estimate=COST,
        name="grad",
    )(place, *pieces, blocks)


def arrange_kernel(place, own, got, potential, out_ref, log_ref):
    c = place[0]
    rows = out_ref.shape[0]

    def mine(v):
        return jnp.where(c == 0, v[:, :rows, :], v[:, rows : 2 * rows, :])

    mine_own, mine_got = mine(own), mine(got)
    low = jnp.where(c == 0, mine_own, mine_got)
    high = jnp.where(c == 0, mine_got, mine_own)
    part = own.shape[2] // 4
    pieces = [v[b, :, j * part : (j + 1) * part] for j in range(4) for v in (low, high) for b in range(4)]
    gradient = jnp.concatenate(pieces, axis=1)
    out_ref[...] = gradient
    scores = (potential[...] - gradient) / entropy
    peak = jnp.max(scores, axis=1, keepdims=True)
    total = jnp.sum(jnp.exp(scores - peak), axis=1, keepdims=True)
    log_ref[...] = peak + jnp.log(total)


def arrange(place, own, got, potential, rows):
    return pl.pallas_call(
        arrange_kernel,
        in_specs=[SMEM, VMEM, VMEM, VMEM],
        out_specs=[VMEM, VMEM],
        out_shape=[
            jax.ShapeDtypeStruct((rows, potential.shape[1]), jnp.float32),
            jax.ShapeDtypeStruct((rows, 1), jnp.float32),
        ],
        compiler_params=params(),
        cost_estimate=COST,
        name="arrange",
    )(place, own, got, potential)


def meet_kernel(*refs):
    refs[-1][...] = jnp.zeros_like(refs[-1])


def meet(flops, width, *arrays):
    return pl.pallas_call(
        meet_kernel,
        in_specs=[pl.BlockSpec(memory_space=pl.ANY)] * len(arrays),
        out_specs=VMEM,
        out_shape=jax.ShapeDtypeStruct((1, width), jnp.float32),
        compiler_params=params(),
        cost_estimate=pl.CostEstimate(flops=flops, bytes_accessed=1000, transcendentals=0),
        name="meet",
    )(*arrays)


def after(value, *others):
    return lax.optimization_barrier((value, *others))[0]


def body(plan, cost_source, cost_target, potential_col, row_mass):
    num_source = plan.shape[0] * NG
    num_target = plan.shape[1] * WIDE
    factor = -2.0 / math.sqrt(num_source * num_target)
    g = lax.axis_index("grp")
    w = lax.axis_index("wide")
    h, y, x, c = coords(w)
    place = jnp.stack([c, x, y, h, g]).astype(jnp.int32)
    plan5 = plan.reshape(NH * NY, NX, NC * cost_source.shape[0], plan.shape[1])

    def wide(v, pairs):
        return lax.ppermute(v, "wide", pairs)

    both = jnp.stack([cost_source, wide(cost_source, CORE_SWAP)])
    costs = [wide(both, column_pairs(d)) for d in (1, 2, 3)]
    halved = split(place, plan5)

    def along_rows(own, got):
        parts = [own[d] + got[d] for d in range(4)]
        return parts[0] + sum(wide(parts[d], row_pairs(d)) for d in (1, 2, 3))

    def finish(total):
        total = total[0] + sum(wide(total[d], column_pairs(d)) for d in (1, 2, 3))
        rows = total.shape[-1] // NH
        return total[..., :rows] + wide(total[..., rows:], H_SWAP)

    near = lax.ppermute(cost_target, "grp", [(i, i ^ 1) for i in range(NG)])
    far = lax.ppermute(cost_target, "grp", [(i, i ^ 2) for i in range(NG)])
    own0, send0 = carry(place, halved, (cost_target,), 1000)
    got0 = wide(send0, CORE_SWAP) + meet(BIG, own0.shape[-1], own0, far, near, *costs)
    last = lax.ppermute(far, "grp", [(i, i ^ 1) for i in range(NG)])
    total0 = along_rows(own0, got0)
    own1, send1 = carry(place, halved, (near, far), BIG)
    total1 = along_rows(own1, wide(send1, CORE_SWAP))
    own2, send2 = carry(place, halved, (after(last, total0),), BIG)
    total2 = along_rows(own2, wide(send2, CORE_SWAP)) + meet(1000, own0.shape[-1], total1)
    blocks = finish(jnp.concatenate([total0, total1, total2], axis=1))

    partial = grad(place, [both] + costs, blocks, factor)
    partial = partial[0] + sum(wide(partial[d], row_pairs(d)) for d in (1, 2, 3))
    parts = lax.all_to_all(partial, ("grp", "wide"), 0, 0, axis_index_groups=GATHER_GROUPS, tiled=True)
    summed = parts.reshape((NG * NH, 4) + parts.shape[1:]).sum(axis=0)
    gradient, log_total = arrange(place, summed, wide(summed, CORE_SWAP), potential_col[None, :], row_mass.shape[0])
    potential_row = entropy * jnp.log(row_mass) - entropy * log_total[:, 0]
    return (gradient, potential_row)


def solution(mesh):
    placed = (P("grp", "wide"), P(("grp", "wide"), None), P("wide", "grp"), P(), P(("grp", "wide")))
    return jax.shard_map(
        body,
        mesh=mesh,
        in_specs=placed,
        out_specs=(P(("grp", "wide"), None), P(("grp", "wide"))),
        check_vma=False,
    )
```

```python
import math

import jax
import jax.numpy as jnp
from jax import lax
from jax.experimental import pallas as pl
from jax.experimental.pallas import tpu as pltpu
from jax.sharding import PartitionSpec as P

entropy = 2.0
NX = NY = 4
NC = 2
NH = 2
NG = 4
WIDE = NH * NY * NX * NC
MIB = 1024 * 1024
BIG = 10**11


def coords(w):
    return w // (NY * NX * NC), (w // (NX * NC)) % NY, (w // NC) % NX, w % NC


def wide_index(h, y, x, c):
    return ((h * NY + y % NY) * NX + x % NX) * NC + c


def wide_pairs(move):
    return [(w, wide_index(*move(*coords(w)))) for w in range(WIDE)]


def row_pairs(d):
    return wide_pairs(lambda h, y, x, c: (h, y, x + d, c) if c == 0 else (h, y + d, x, c))


def column_pairs(d):
    return wide_pairs(lambda h, y, x, c: (h, y + d, x, c) if c == 0 else (h, y, x + d, c))


CORE_SWAP = wide_pairs(lambda h, y, x, c: (h, y, x, 1 - c))
H_SWAP = wide_pairs(lambda h, y, x, c: (1 - h, y, x, c))
GATHER_GROUPS = [
    [
        g * WIDE + (wide_index(h, b, a, 0) if c == 0 else wide_index(h, a, b, 1))
        for g in range(NG)
        for h in range(NH)
        for b in range(4)
    ]
    for c in range(NC)
    for a in range(4)
]


def halves(v):
    hi = v.astype(jnp.bfloat16)
    return hi, (v - hi.astype(jnp.float32)).astype(jnp.bfloat16)


def dot3(a, b):
    def dot(u, v):
        return jnp.dot(u, v, preferred_element_type=jnp.float32)

    return dot(a[0], b[0]) + (dot(a[0], b[1]) + dot(a[1], b[0]))


def params():
    return pltpu.CompilerParams(vmem_limit_bytes=40 * MIB)


COST = pl.CostEstimate(flops=1000, bytes_accessed=1000, transcendentals=0)
VMEM = pl.BlockSpec(memory_space=pltpu.VMEM)
SMEM = pl.BlockSpec(memory_space=pltpu.SMEM)


def split_kernel(place, plan_ref, hi_ref, lo_ref):
    h = place[3]
    groups, nx, run, depth = plan_ref.shape
    per = groups // NH
    for xx in range(nx):
        for dh in range(NH):
            for i in range(per):
                hi, lo = halves(plan_ref[lax.rem(h + dh, NH) * per + i, xx])
                at = (dh * per + i) * run
                hi_ref[xx, at : at + run, :] = hi
                lo_ref[xx, at : at + run, :] = lo


def split(place, plan5):
    groups, nx, run, depth = plan5.shape
    out = jax.ShapeDtypeStruct((nx, groups * run, depth), jnp.bfloat16)
    return pl.pallas_call(
        split_kernel,
        in_specs=[SMEM, VMEM],
        out_specs=[VMEM, VMEM],
        out_shape=[out, out],
        compiler_params=params(),
        cost_estimate=COST,
        name="split",
    )(place, plan5)


def carry_kernel(place, hi_ref, lo_ref, *refs):
    blocks, (own_ref, send_ref, held) = refs[:-3], refs[-3:]
    c, x, y = place[0], place[1], place[2]
    nx, rows, _ = hi_ref.shape
    per = rows // (NH * NY)
    for n, block in enumerate(blocks):
        right = halves(block[...])
        half = block.shape[1] // NC
        part = half // 4
        for xx in range(nx):
            out = dot3((hi_ref[xx], lo_ref[xx]), right)
            for i in range(NH * NY):
                held[n, i, xx] = out[i * per : (i + 1) * per]
        for ref, core in ((own_ref, c), (send_ref, 1 - c)):
            a, b = jnp.where(core == 0, x, y), jnp.where(core == 0, y, x)
            lanes = pl.ds(pl.multiple_of(core * half, half), half)
            for i in range(4):
                tiles = []
                for dh in range(NH):
                    for j in range(4):
                        yy, xx = jnp.where(core == 0, j, i), jnp.where(core == 0, i, j)
                        tiles.append(held[n, dh * NY + yy, xx, :, lanes])
                turned = jnp.concatenate(tiles, axis=0).T
                for j in range(4):
                    ref[lax.rem(i - a + 4, 4), lax.rem(j - b + 4, 4), n] = turned[j * part : (j + 1) * part]
def carry(place, plan, blocks, flops):
    nx, rows, _ = plan[0].shape
    cols = blocks[0].shape[1]
    out = jax.ShapeDtypeStruct((4, 4, len(blocks), cols // (NC * 4), rows), jnp.float32)
    return pl.pallas_call(
        carry_kernel,
        in_specs=[SMEM, VMEM, VMEM] + [VMEM] * len(blocks),
        out_specs=[VMEM, VMEM],
        out_shape=[out, out],
        scratch_shapes=[pltpu.VMEM((len(blocks), NH * NY, nx, rows // (NH * NY), cols), jnp.float32)],
        compiler_params=params(),
        cost_estimate=pl.CostEstimate(flops=flops, bytes_accessed=1000, transcendentals=0),
        name="carry",
    )(place, *plan, *blocks)


def grad_kernel(place, *refs, factor):
    pieces, (blocks, out_ref, cost, held, full) = refs[:4], refs[4:]
    c, x, y, g = place[0], place[1], place[2], place[4]
    a, b = jnp.where(c == 0, x, y), jnp.where(c == 0, y, x)
    run = pieces[0].shape[1]
    for d in range(4):
        bb = lax.rem(b - d + 4, 4)
        for dc in range(NC):
            at = (bb * NC + lax.rem(c + dc, NC)) * run
            cost[pl.ds(pl.multiple_of(at, run), run), :] = pieces[d][dc]
    part = blocks.shape[1]
    low, even = g < 2, lax.rem(g, 2) == 0
    near = jnp.where(even, g + 1, g - 1)
    order = [g, near, jnp.where(low, g + 2, g - 2), jnp.where(low, near + 2, near - 2)]
    for k, j in enumerate(order):
        held[pl.ds(pl.multiple_of(j * part, part), part), :] = blocks[k]
    left = halves(held[...])
    step = 512
    width = cost.shape[1]
    for at in range(0, width, step):
        full[at : at + step, :] = factor * dot3(left, halves(cost[:, at : at + step])).T
    chips = NG * NH * NY * NX
    rows = width // chips
    for cc in range(NC):

        @pl.when(c == cc)
        def _(cc=cc):
            for o in range(chips):
                gh, yy, xx = o // (NY * NX), (o // NX) % NY, o % NX
                aa, bb = (xx, yy) if cc == 0 else (yy, xx)
                at = (gh * 4 + bb) * rows
                out_ref[lax.rem(aa - a + 4, 4), at : at + rows, :] = full[o * rows : (o + 1) * rows, :]


def grad(place, pieces, blocks, factor):
    _, run, width = pieces[0].shape
    rows = NC * 4 * run
    cols = blocks.shape[0] * blocks.shape[1]
    return pl.pallas_call(
        lambda place, *refs: grad_kernel(place, *refs, factor=factor),
        in_specs=[SMEM] + [VMEM] * 5,
        out_specs=VMEM,
        out_shape=jax.ShapeDtypeStruct((4, width // 4, cols), jnp.float32),
        scratch_shapes=[
            pltpu.VMEM((rows, width), jnp.float32),
            pltpu.VMEM((cols, rows), jnp.float32),
            pltpu.VMEM((width, cols), jnp.float32),
        ],
        compiler_params=params(),
        cost_estimate=COST,
        name="grad",
    )(place, *pieces, blocks)


def arrange_kernel(place, own, got, potential, out_ref, log_ref):
    c = place[0]
    rows = out_ref.shape[0]

    def mine(v):
        return jnp.where(c == 0, v[:, :rows, :], v[:, rows : 2 * rows, :])

    mine_own, mine_got = mine(own), mine(got)
    low = jnp.where(c == 0, mine_own, mine_got)
    high = jnp.where(c == 0, mine_got, mine_own)
    part = own.shape[2] // 4
    pieces = [v[b, :, j * part : (j + 1) * part] for j in range(4) for v in (low, high) for b in range(4)]
    gradient = jnp.concatenate(pieces, axis=1)
    out_ref[...] = gradient
    scores = (potential[...] - gradient) / entropy
    peak = jnp.max(scores, axis=1, keepdims=True)
    total = jnp.sum(jnp.exp(scores - peak), axis=1, keepdims=True)
    log_ref[...] = peak + jnp.log(total)


def arrange(place, own, got, potential, rows):
    return pl.pallas_call(
        arrange_kernel,
        in_specs=[SMEM, VMEM, VMEM, VMEM],
        out_specs=[VMEM, VMEM],
        out_shape=[
            jax.ShapeDtypeStruct((rows, potential.shape[1]), jnp.float32),
            jax.ShapeDtypeStruct((rows, 1), jnp.float32),
        ],
        compiler_params=params(),
        cost_estimate=COST,
        name="arrange",
    )(place, own, got, potential)


def meet_kernel(*refs):
    refs[-1][...] = jnp.zeros_like(refs[-1])


def meet(flops, width, *arrays):
    return pl.pallas_call(
        meet_kernel,
        in_specs=[pl.BlockSpec(memory_space=pl.ANY)] * len(arrays),
        out_specs=VMEM,
        out_shape=jax.ShapeDtypeStruct((1, width), jnp.float32),
        compiler_params=params(),
        cost_estimate=pl.CostEstimate(flops=flops, bytes_accessed=1000, transcendentals=0),
        name="meet",
    )(*arrays)


def after(value, *others):
    return lax.optimization_barrier((value, *others))[0]


def body(plan, cost_source, cost_target, potential_col, row_mass):
    num_source = plan.shape[0] * NG
    num_target = plan.shape[1] * WIDE
    factor = -2.0 / math.sqrt(num_source * num_target)
    g = lax.axis_index("grp")
    w = lax.axis_index("wide")
    h, y, x, c = coords(w)
    place = jnp.stack([c, x, y, h, g]).astype(jnp.int32)
    plan5 = plan.reshape(NH * NY, NX, NC * cost_source.shape[0], plan.shape[1])

    def wide(v, pairs):
        return lax.ppermute(v, "wide", pairs)

    both = jnp.stack([cost_source, wide(cost_source, CORE_SWAP)])
    costs = [wide(both, column_pairs(d)) for d in (1, 2, 3)]
    halved = split(place, plan5)

    def along_rows(own, got):
        parts = [own[d] + got[d] for d in range(4)]
        return parts[0] + sum(wide(parts[d], row_pairs(d)) for d in (1, 2, 3))

    def finish(total):
        total = total[0] + sum(wide(total[d], column_pairs(d)) for d in (1, 2, 3))
        rows = total.shape[-1] // NH
        return total[..., :rows] + wide(total[..., rows:], H_SWAP)

    near = lax.ppermute(cost_target, "grp", [(i, i ^ 1) for i in range(NG)])
    far = lax.ppermute(cost_target, "grp", [(i, i ^ 2) for i in range(NG)])
    own0, send0 = carry(place, halved, (cost_target,), 1000)
    got0 = wide(send0, CORE_SWAP) + meet(BIG, own0.shape[-1], own0, far, near, *costs)
    last = lax.ppermute(far, "grp", [(i, i ^ 1) for i in range(NG)])
    total0 = along_rows(own0, got0)
    own1, send1 = carry(place, halved, (near, far), BIG)
    total1 = along_rows(own1, wide(send1, CORE_SWAP))
    own2, send2 = carry(place, halved, (after(last, total0),), BIG)
    total2 = along_rows(own2, wide(send2, CORE_SWAP)) + meet(1000, own0.shape[-1], total1)
    blocks = finish(jnp.concatenate([total0, total1, total2], axis=1))

    partial = grad(place, [both] + costs, blocks, factor)
    partial = partial[0] + sum(wide(partial[d], row_pairs(d)) for d in (1, 2, 3))
    partial = partial.reshape(NG * NH * 4, -1, partial.shape[-1])
    parts = lax.all_to_all(partial, ("grp", "wide"), 0, 0, axis_index_groups=GATHER_GROUPS, tiled=True)
    summed = parts.reshape((NG * NH, 4) + parts.shape[1:]).sum(axis=0)
    gradient, log_total = arrange(place, summed, wide(summed, CORE_SWAP), potential_col[None, :], row_mass.shape[0])
    potential_row = entropy * jnp.log(row_mass) - entropy * log_total[:, 0]
    return (gradient, potential_row)


def solution(mesh):
    placed = (P("grp", "wide"), P(("grp", "wide"), None), P("wide", "grp"), P(), P(("grp", "wide")))
    return jax.shard_map(
        body,
        mesh=mesh,
        in_specs=placed,
        out_specs=(P(("grp", "wide"), None), P(("grp", "wide"))),
        check_vma=False,
    )
```

```python
import math

import jax
import jax.numpy as jnp
from jax import lax
from jax.experimental import pallas as pl
from jax.experimental.pallas import tpu as pltpu
from jax.sharding import PartitionSpec as P

entropy = 2.0
NX = NY = 4
NC = 2
NH = 2
NG = 4
WIDE = NH * NY * NX * NC
MIB = 1024 * 1024
BIG = 10**11


def coords(w):
    return w // (NY * NX * NC), (w // (NX * NC)) % NY, (w // NC) % NX, w % NC


def wide_index(h, y, x, c):
    return ((h * NY + y % NY) * NX + x % NX) * NC + c


def wide_pairs(move):
    return [(w, wide_index(*move(*coords(w)))) for w in range(WIDE)]


def row_pairs(d):
    return wide_pairs(lambda h, y, x, c: (h, y, x + d, c) if c == 0 else (h, y + d, x, c))


def column_pairs(d):
    return wide_pairs(lambda h, y, x, c: (h, y + d, x, c) if c == 0 else (h, y, x + d, c))


CORE_SWAP = wide_pairs(lambda h, y, x, c: (h, y, x, 1 - c))
H_SWAP = wide_pairs(lambda h, y, x, c: (1 - h, y, x, c))
GATHER_GROUPS = [
    [
        g * WIDE + (wide_index(h, b, a, 0) if c == 0 else wide_index(h, a, b, 1))
        for g in range(NG)
        for h in range(NH)
        for b in range(4)
    ]
    for c in range(NC)
    for a in range(4)
]


def halves(v):
    hi = v.astype(jnp.bfloat16)
    return hi, (v - hi.astype(jnp.float32)).astype(jnp.bfloat16)


def dot3(a, b):
    def dot(u, v):
        return jnp.dot(u, v, preferred_element_type=jnp.float32)

    return dot(a[0], b[0]) + (dot(a[0], b[1]) + dot(a[1], b[0]))


def params():
    return pltpu.CompilerParams(vmem_limit_bytes=40 * MIB)


COST = pl.CostEstimate(flops=1000, bytes_accessed=1000, transcendentals=0)
VMEM = pl.BlockSpec(memory_space=pltpu.VMEM)
SMEM = pl.BlockSpec(memory_space=pltpu.SMEM)


def split_kernel(place, plan_ref, hi_ref, lo_ref):
    h = place[3]
    groups, nx, run, depth = plan_ref.shape
    per = groups // NH
    for xx in range(nx):
        for dh in range(NH):
            for i in range(per):
                hi, lo = halves(plan_ref[lax.rem(h + dh, NH) * per + i, xx])
                at = (dh * per + i) * run
                hi_ref[xx, at : at + run, :] = hi
                lo_ref[xx, at : at + run, :] = lo


def split(place, plan5):
    groups, nx, run, depth = plan5.shape
    out = jax.ShapeDtypeStruct((nx, groups * run, depth), jnp.bfloat16)
    return pl.pallas_call(
        split_kernel,
        in_specs=[SMEM, VMEM],
        out_specs=[VMEM, VMEM],
        out_shape=[out, out],
        compiler_params=params(),
        cost_estimate=COST,
        name="split",
    )(place, plan5)


def carry_kernel(place, hi_ref, lo_ref, *refs):
    blocks, (own_ref, send_ref, held) = refs[:-3], refs[-3:]
    c, x, y = place[0], place[1], place[2]
    nx, rows, _ = hi_ref.shape
    per = rows // (NH * NY)
    for n, block in enumerate(blocks):
        right = halves(block[...])
        half = block.shape[1] // NC
        part = half // 4
        for xx in range(nx):
            out = dot3((hi_ref[xx], lo_ref[xx]), right)
            for i in range(NH * NY):
                held[n, i, xx] = out[i * per : (i + 1) * per]
        for ref, core in ((own_ref, c), (send_ref, 1 - c)):
            a, b = jnp.where(core == 0, x, y), jnp.where(core == 0, y, x)
            lanes = pl.ds(pl.multiple_of(core * half, half), half)
            for i in range(4):
                tiles = []
                for dh in range(NH):
                    for j in range(4):
                        yy, xx = jnp.where(core == 0, j, i), jnp.where(core == 0, i, j)
                        tiles.append(held[n, dh * NY + yy, xx, :, lanes])
                turned = jnp.concatenate(tiles, axis=0).T
                for j in range(4):
                    ref[lax.rem(i - a + 4, 4), lax.rem(j - b + 4, 4), n] = turned[j * part : (j + 1) * part]
def carry(place, plan, blocks, flops):
    nx, rows, _ = plan[0].shape
    cols = blocks[0].shape[1]
    out = jax.ShapeDtypeStruct((4, 4, len(blocks), cols // (NC * 4), rows), jnp.float32)
    return pl.pallas_call(
        carry_kernel,
        in_specs=[SMEM, VMEM, VMEM] + [VMEM] * len(blocks),
        out_specs=[VMEM, VMEM],
        out_shape=[out, out],
        scratch_shapes=[pltpu.VMEM((len(blocks), NH * NY, nx, rows // (NH * NY), cols), jnp.float32)],
        compiler_params=params(),
        cost_estimate=pl.CostEstimate(flops=flops, bytes_accessed=1000, transcendentals=0),
        name="carry",
    )(place, *plan, *blocks)


def grad_kernel(place, *refs, factor):
    pieces, (blocks, out_ref, cost, held, full) = refs[:4], refs[4:]
    c, x, y, g = place[0], place[1], place[2], place[4]
    a, b = jnp.where(c == 0, x, y), jnp.where(c == 0, y, x)
    run = pieces[0].shape[1]
    for d in range(4):
        bb = lax.rem(b - d + 4, 4)
        for dc in range(NC):
            at = (bb * NC + lax.rem(c + dc, NC)) * run
            cost[pl.ds(pl.multiple_of(at, run), run), :] = pieces[d][dc]
    part = blocks.shape[1]
    low, even = g < 2, lax.rem(g, 2) == 0
    near = jnp.where(even, g + 1, g - 1)
    order = [g, near, jnp.where(low, g + 2, g - 2), jnp.where(low, near + 2, near - 2)]
    for k, j in enumerate(order):
        held[pl.ds(pl.multiple_of(j * part, part), part), :] = blocks[k]
    left = halves(held[...])
    step = 512
    width = cost.shape[1]
    for at in range(0, width, step):
        full[at : at + step, :] = factor * dot3(left, halves(cost[:, at : at + step])).T
    chips = NG * NH * NY * NX
    rows = width // chips
    for cc in range(NC):

        @pl.when(c == cc)
        def _(cc=cc):
            for o in range(chips):
                gh, yy, xx = o // (NY * NX), (o // NX) % NY, o % NX
                aa, bb = (xx, yy) if cc == 0 else (yy, xx)
                at = (gh * 4 + bb) * rows
                out_ref[lax.rem(aa - a + 4, 4), at : at + rows, :] = full[o * rows : (o + 1) * rows, :]


def grad(place, pieces, blocks, factor):
    _, run, width = pieces[0].shape
    rows = NC * 4 * run
    cols = blocks.shape[0] * blocks.shape[1]
    return pl.pallas_call(
        lambda place, *refs: grad_kernel(place, *refs, factor=factor),
        in_specs=[SMEM] + [VMEM] * 5,
        out_specs=VMEM,
        out_shape=jax.ShapeDtypeStruct((4, width // 4, cols), jnp.float32),
        scratch_shapes=[
            pltpu.VMEM((rows, width), jnp.float32),
            pltpu.VMEM((cols, rows), jnp.float32),
            pltpu.VMEM((width, cols), jnp.float32),
        ],
        compiler_params=params(),
        cost_estimate=COST,
        name="grad",
    )(place, *pieces, blocks)


def arrange_kernel(place, own, got, potential, out_ref, log_ref):
    c = place[0]
    rows = out_ref.shape[0]

    def mine(v):
        return jnp.where(c == 0, v[:, :rows, :], v[:, rows : 2 * rows, :])

    mine_own, mine_got = mine(own), mine(got)
    low = jnp.where(c == 0, mine_own, mine_got)
    high = jnp.where(c == 0, mine_got, mine_own)
    part = own.shape[2] // 4
    pieces = [v[b, :, j * part : (j + 1) * part] for j in range(4) for v in (low, high) for b in range(4)]
    gradient = jnp.concatenate(pieces, axis=1)
    out_ref[...] = gradient
    scores = (potential[...] - gradient) / entropy
    peak = jnp.max(scores, axis=1, keepdims=True)
    total = jnp.sum(jnp.exp(scores - peak), axis=1, keepdims=True)
    log_ref[...] = peak + jnp.log(total)


def arrange(place, own, got, potential, rows):
    return pl.pallas_call(
        arrange_kernel,
        in_specs=[SMEM, VMEM, VMEM, VMEM],
        out_specs=[VMEM, VMEM],
        out_shape=[
            jax.ShapeDtypeStruct((rows, potential.shape[1]), jnp.float32),
            jax.ShapeDtypeStruct((rows, 1), jnp.float32),
        ],
        compiler_params=params(),
        cost_estimate=COST,
        name="arrange",
    )(place, own, got, potential)


def meet_kernel(*refs):
    refs[-1][...] = jnp.zeros_like(refs[-1])


def meet(flops, width, *arrays):
    return pl.pallas_call(
        meet_kernel,
        in_specs=[pl.BlockSpec(memory_space=pl.ANY)] * len(arrays),
        out_specs=VMEM,
        out_shape=jax.ShapeDtypeStruct((1, width), jnp.float32),
        compiler_params=params(),
        cost_estimate=pl.CostEstimate(flops=flops, bytes_accessed=1000, transcendentals=0),
        name="meet",
    )(*arrays)


def after(value, *others):
    return lax.optimization_barrier((value, *others))[0]


def body(plan, cost_source, cost_target, potential_col, row_mass):
    num_source = plan.shape[0] * NG
    num_target = plan.shape[1] * WIDE
    factor = -2.0 / math.sqrt(num_source * num_target)
    g = lax.axis_index("grp")
    w = lax.axis_index("wide")
    h, y, x, c = coords(w)
    place = jnp.stack([c, x, y, h, g]).astype(jnp.int32)
    plan5 = plan.reshape(NH * NY, NX, NC * cost_source.shape[0], plan.shape[1])

    def wide(v, pairs):
        return lax.ppermute(v, "wide", pairs)

    both = jnp.stack([cost_source, wide(cost_source, CORE_SWAP)])
    costs = [wide(both, column_pairs(d)) for d in (1, 2, 3)]
    halved = split(place, plan5)

    def along_rows(own, got):
        parts = [own[d] + got[d] for d in range(4)]
        return parts[0] + sum(wide(parts[d], row_pairs(d)) for d in (2, 1, 3))

    def finish(total):
        total = total[0] + sum(wide(total[d], column_pairs(d)) for d in (2, 1, 3))
        rows = total.shape[-1] // NH
        return total[..., :rows] + wide(total[..., rows:], H_SWAP)

    near = lax.ppermute(cost_target, "grp", [(i, i ^ 1) for i in range(NG)])
    far = lax.ppermute(cost_target, "grp", [(i, i ^ 2) for i in range(NG)])
    own0, send0 = carry(place, halved, (cost_target,), 1000)
    got0 = wide(send0, CORE_SWAP) + meet(BIG, own0.shape[-1], own0, far, near, *costs)
    last = lax.ppermute(far, "grp", [(i, i ^ 1) for i in range(NG)])
    total0 = along_rows(own0, got0)
    own1, send1 = carry(place, halved, (near, far), BIG)
    total1 = along_rows(own1, wide(send1, CORE_SWAP))
    own2, send2 = carry(place, halved, (after(last, total0),), BIG)
    total2 = along_rows(own2, wide(send2, CORE_SWAP)) + meet(1000, own0.shape[-1], total1)
    blocks = finish(jnp.concatenate([total0, total1, total2], axis=1))

    partial = grad(place, [both] + costs, blocks, factor)
    partial = partial[0] + sum(wide(partial[d], row_pairs(d)) for d in (2, 1, 3))
    partial = partial.reshape(NG * NH * 4, -1, partial.shape[-1])
    parts = lax.all_to_all(partial, ("grp", "wide"), 0, 0, axis_index_groups=GATHER_GROUPS, tiled=True)
    summed = parts.reshape((NG * NH, 4) + parts.shape[1:]).sum(axis=0)
    gradient, log_total = arrange(place, summed, wide(summed, CORE_SWAP), potential_col[None, :], row_mass.shape[0])
    potential_row = entropy * jnp.log(row_mass) - entropy * log_total[:, 0]
    return (gradient, potential_row)


def solution(mesh):
    placed = (P("grp", "wide"), P(("grp", "wide"), None), P("wide", "grp"), P(), P(("grp", "wide")))
    return jax.shard_map(
        body,
        mesh=mesh,
        in_specs=placed,
        out_specs=(P(("grp", "wide"), None), P(("grp", "wide"))),
        check_vma=False,
    )
```
